32 devices in a mesh: groups: 2 (over y), dec: 16 (over z, x, core).
Axes of the slice: x: 2, y: 2, z: 4, core: 2. Of those that a mesh axis runs over, the one named last changes fastest.
Arguments:
- panels: bfloat16 [512, 64, 512], P(('groups', 'dec')), parts along dimension 0, may hold values from -6 to 6
- tile_panels: int32 [128, 16], P(('groups', 'dec')), parts along dimension 0, may hold values from 0 to 255, as said below
- tile_count: int32 [32], P(('groups', 'dec')), parts along dimension 0, may hold values from 1 to 4, as said below
- conv_weight: bfloat16 [3, 3, 3, 512, 256], replicated, may hold values from -0.0546875 to 0.0546875
- conv_bias: float32 [256], replicated, may hold values from -4 to 4
- norm_gain: float32 [256], replicated, may hold values from 0.1 to 1.9
- norm_shift: float32 [256], replicated, may hold values from -3 to 3
Outputs:
- decoded: bfloat16 [128, 392, 256], P(('groups', 'dec')), parts along dimension 0
The draws below stay inside these ranges and needn't reach their ends.
There are 2 independent parts, one for each index of `groups`. The reference program is written for one: setup_inputs(seed, part) draws one part's arguments, and reference() takes and returns one part's arrays. A program takes and returns all parts, laid end to end along the dimension named above; an argument that names none is the same for every part. Nothing has to cross between parts.
Inputs may be any that keep to these rules, and one draw needn't show every extreme that they name: `tile_panels`: panel p lies on device p // 16. Over all 4 rows of one device, at most 4 entries name panels of any one device, repeats counted; in every draw each device's rows name exactly 4 panels on each of 16 devices. `tile_count`: in every draw some device has 4 live rows.
All inputs are finite; a program needn't handle non-finite values.
Results may differ from the reference program's by a relative error of at most 0.001.
Values may be sent and summed in bfloat16 or wider, within the bound.
A program may use at most 128 MiB of HBM per device.

```python
import jax
import jax.numpy as jnp
from jax import lax

C_IN = 512
C_OUT = 256
GROUPS = 32
PH = 8
PW = 8
GH = 2
GW = 2
TILE_DEV = 4
PAN_DEV = 16
DECODERS = 16
WT = 4
CELLS = 64
OCELLS = 392
SLOTS = 16
TILES = 64
PANELS = 256
CAP = 4


def permute_row(row_key, values):
    return jax.random.permutation(row_key, values)


def owner_order(row_key):
    return jax.random.permutation(row_key, DECODERS)


def draw_tile_panels(key, part):
    refs_total = TILE_DEV * SLOTS
    order_keys = jax.random.split(jax.random.fold_in(key, 1), DECODERS)
    owners_perm = jax.vmap(owner_order)(order_keys)
    group_of = jnp.arange(refs_total, dtype=jnp.int32) // CAP
    owner_dev = owners_perm[:, group_of]
    local_row = jax.random.randint(jax.random.fold_in(key, 2), (DECODERS, refs_total), 0, PAN_DEV)
    panel_id = owner_dev * PAN_DEV + local_row
    shuffle_keys = jax.random.split(jax.random.fold_in(key, 3), DECODERS)
    shuffled = jax.vmap(permute_row)(shuffle_keys, panel_id)
    return shuffled.reshape(DECODERS * TILE_DEV, SLOTS).astype(jnp.int32)


def draw_tile_count(key, part):
    first_key = jax.random.fold_in(key, 1)
    second_key = jax.random.fold_in(key, 2)
    third_key = jax.random.fold_in(key, 3)
    lottery = jax.random.randint(first_key, (DECODERS,), 0, 10)
    modest = 1 + jax.random.randint(second_key, (DECODERS,), 0, max(1, TILE_DEV // 2))
    counts = jnp.where(lottery < 2, TILE_DEV, modest)
    picked_dev = jax.random.randint(third_key, (), 0, DECODERS)
    return jnp.where(jnp.arange(DECODERS) == picked_dev, TILE_DEV, counts).astype(jnp.int32)


def steps_of(rng, shape, shards, smallest, top_value):
    factor_of, own = 1.0, jax.random.fold_in(rng, 6)
    for dim, parts in shards:
        steps = jnp.exp(jax.random.uniform(jax.random.fold_in(own, dim), (parts,), jnp.float32, smallest / len(shards), top_value / len(shards)))
        factor_of = factor_of * jnp.repeat(steps, shape[dim] // parts).reshape([-1 if axis == dim else 1 for axis in range(len(shape))])
    return factor_of


def scatter_about(key, shape, deviation, limit, shards=(), held_as=jnp.bfloat16):
    drawn = deviation * jax.random.normal(key, shape, jnp.float32)
    if shards:
        drawn = drawn * steps_of(key, shape, shards, -0.22, 0.18)
    return jnp.clip(drawn, -limit, limit).astype(held_as)


def setup_inputs(seed: int = 0, part: int = 0) -> dict:
    key_list = jax.random.split(jax.random.key(seed), 8)
    part_keys = jax.random.split(jax.random.fold_in(key_list[7], part), 8)
    return {
        "panels": scatter_about(part_keys[0], (PANELS, CELLS, C_IN), 1.0, 6.0, ((0, 16),)),
        "tile_panels": draw_tile_panels(jax.random.fold_in(jax.random.fold_in(key_list[7], part), 71), part),
        "tile_count": draw_tile_count(jax.random.fold_in(jax.random.fold_in(key_list[7], part), 71), part),
        "conv_weight": scatter_about(key_list[3], (3, 3, 3, C_IN, C_OUT), (27 * C_IN) ** -0.5, 0.0546875),
        "conv_bias": scatter_about(key_list[4], (C_OUT,), 1.0, 4.0, (), jnp.float32),
        "norm_gain": jnp.clip(1.0 + 0.18 * jax.random.normal(key_list[5], (C_OUT,), jnp.float32), 0.1, 1.9),
        "norm_shift": scatter_about(key_list[6], (C_OUT,), 0.5, 3.0, (), jnp.float32),
    }


epsilon = 1e-06

def arrange_window(panel_rows, frame_count, grid_high, grid_wide, panel_high, panel_wide):
    channels = panel_rows.shape[-1]
    blocks = panel_rows.reshape(frame_count, grid_high, grid_wide, panel_high, panel_wide, channels)
    blocks = blocks.transpose(0, 1, 3, 2, 4, 5)
    return blocks.reshape(frame_count, grid_high * panel_high, grid_wide * panel_wide, channels)

def decode_window(window, kernel, conv_bias, norm_gain, norm_shift, groups):
    out_frames = window.shape[0] - 2
    out_high = window.shape[1] - 2
    out_wide = window.shape[2] - 2
    pieces = []
    for tap_t in range(3):
        for tap_h in range(3):
            for tap_w in range(3):
                pieces.append(window[tap_t:tap_t + out_frames, tap_h:tap_h + out_high, tap_w:tap_w + out_wide, :])
    columns = jnp.concatenate(pieces, axis=-1)
    columns = columns.reshape(out_frames * out_high * out_wide, columns.shape[-1])
    conv_out = jnp.dot(columns, kernel, preferred_element_type=jnp.float32) + conv_bias.astype(jnp.float32)
    cell_count = conv_out.shape[0]
    width_out = conv_out.shape[1]
    grouped = conv_out.reshape(cell_count, groups, width_out // groups)
    center = lax.optimization_barrier(jnp.mean(grouped, axis=(0, 2), keepdims=True))
    shifted = grouped - center
    spread = lax.optimization_barrier(jnp.mean(shifted * shifted, axis=(0, 2), keepdims=True))
    normed = (shifted / jnp.sqrt(spread + epsilon)).reshape(cell_count, width_out)
    scaled = normed * norm_gain.astype(jnp.float32) + norm_shift.astype(jnp.float32)
    return jax.nn.silu(scaled).astype(jnp.bfloat16)

def reference(panels, tile_panels, tile_count, conv_weight, conv_bias, norm_gain, norm_shift):
    kernel = conv_weight.reshape(27 * C_IN, C_OUT)
    tile_index = jnp.arange(TILES, dtype=jnp.int32)
    alive = tile_index % TILE_DEV < tile_count[tile_index // TILE_DEV]

    def single(inputs):
        panel_ids, is_live = inputs

        def active(chosen_ids):
            window = arrange_window(panels[chosen_ids], WT, GH, GW, PH, PW)
            return decode_window(window, kernel, conv_bias, norm_gain, norm_shift, GROUPS)

        def resting(chosen_ids):
            return jnp.zeros((OCELLS, C_OUT), jnp.bfloat16)
        return lax.cond(is_live, active, resting, panel_ids)
    return lax.map(single, (tile_panels, alive))
```

```python
import jax
import jax.numpy as jnp
from jax import lax
from jax.experimental import pallas as pl
from jax.experimental.pallas import tpu as pltpu
from jax.sharding import PartitionSpec as P

C_OUT = 256
GROUPS = 32
PH = 8
PW = 8
GH = 2
GW = 2
WT = 4
OCELLS = 392
ROW = GW * PW
OH = GH * PH - 2
OW = GW * PW - 2
OF = WT - 2
MROWS = OF * OH * ROW

epsilon = 1e-06


def pick_kernel(rows, panels, out, sem):
    count = out.shape[0]
    for i in range(count):
        pltpu.make_async_copy(panels.at[rows[i]], out.at[i], sem).start()
    pltpu.make_async_copy(out, out, sem).wait()


def pick_rows(panels, rows):
    return pl.pallas_call(
        pick_kernel,
        out_shape=jax.ShapeDtypeStruct((rows.shape[0], *panels.shape[1:]), panels.dtype),
        grid_spec=pltpu.PrefetchScalarGridSpec(
            num_scalar_prefetch=1,
            grid=(1,),
            in_specs=[pl.BlockSpec(memory_space=pl.ANY)],
            out_specs=pl.BlockSpec(memory_space=pl.ANY),
            scratch_shapes=[pltpu.SemaphoreType.DMA],
        ),
    )(rows, panels)


def fetch_panels(panels, work_rows, live_tiles, capacity):
    devices = lax.axis_size("dec")
    per_device = panels.shape[0]
    tile_rows, slot_count = work_rows.shape
    wanted = work_rows.reshape(tile_rows * slot_count)
    ref_live = jnp.arange(tile_rows * slot_count, dtype=jnp.int32) // slot_count < live_tiles
    owner_dev = wanted // per_device
    local_row = wanted % per_device
    order = jnp.arange(tile_rows * slot_count, dtype=jnp.int32)
    earlier = (owner_dev[:, None] == owner_dev[None, :]) & (order[None, :] < order[:, None])
    slot_rank = jnp.sum(earlier.astype(jnp.int32), axis=1)
    where_to = owner_dev * capacity + slot_rank
    places = jnp.arange(devices * capacity, dtype=jnp.int32)
    here = (where_to[None, :] == places[:, None]) & ref_live[None, :]
    request = jnp.sum(jnp.where(here, local_row[None, :], 0), axis=1)
    asked_rows = lax.all_to_all(
        request.reshape(devices, capacity), "dec", split_axis=0, concat_axis=0, tiled=True
    )
    picked = pick_rows(panels, asked_rows.reshape(-1))
    picked = picked.reshape(devices, capacity, *panels.shape[1:])
    returned = lax.all_to_all(picked, "dec", split_axis=0, concat_axis=0, tiled=True)
    landed = returned.reshape(devices * capacity, panels.shape[1], panels.shape[2])
    return landed, jnp.where(ref_live, where_to, 0)


def decode_kernel(idx, count, panels, weight, bias, gain, shift, out, stage, win, cols, flat, sems):
    tile = pl.program_id(0)
    slots = stage.shape[1]
    live = count[0]

    def fetch(which, slot):
        for s in range(slots):
            pltpu.make_async_copy(
                panels.at[idx[which * slots + s]], stage.at[slot, s], sems.at[slot]
            ).start()

    @pl.when(tile == 0)
    def _():
        fetch(0, 0)

    @pl.when(tile + 1 < live)
    def _():
        fetch(tile + 1, (tile + 1) % 2)

    @pl.when(tile < live)
    def _():
        slot = tile % 2
        pltpu.make_async_copy(stage.at[slot], stage.at[slot], sems.at[slot]).wait()
        channels = stage.shape[3]
        for f in range(WT):
            for g in range(GH):
                halves = [
                    stage[slot, (f * GH + g) * GW + h].astype(jnp.float32).reshape(PH, PW, channels)
                    for h in range(GW)
                ]
                rows = jnp.concatenate(halves, axis=1).reshape(PH * ROW, channels)
                win[f, pl.ds(g * PH * ROW, PH * ROW), :] = rows.astype(jnp.bfloat16)
        for a in range(3):
            for b in range(3):
                for f in range(OF):
                    cols[pl.ds(f * OH * ROW, OH * ROW), pl.ds((a * 3 + b) * channels, channels)] = win[
                        f + a, pl.ds(b * ROW, OH * ROW), :
                    ]
        conv = jnp.dot(cols[...], weight[0], preferred_element_type=jnp.float32)
        for c in (1, 2):
            part = jnp.dot(cols[...], weight[c], preferred_element_type=jnp.float32)
            conv = conv + pltpu.roll(part, MROWS - c, 0)
        conv = conv + bias[...]
        column = lax.broadcasted_iota(jnp.int32, (MROWS, C_OUT), 0) % ROW
        valid = column < OW
        lane = lax.broadcasted_iota(jnp.int32, (C_OUT, C_OUT), 0) // (C_OUT // GROUPS)
        other = lax.broadcasted_iota(jnp.int32, (C_OUT, C_OUT), 1) // (C_OUT // GROUPS)
        same = jnp.where(lane == other, 1.0, 0.0).astype(jnp.float32)
        cells = OCELLS * (C_OUT // GROUPS)

        def group_mean(x):
            total = jnp.sum(jnp.where(valid, x, 0.0), axis=0, keepdims=True)
            total = jnp.broadcast_to(total, (8, C_OUT))
            total = jnp.dot(
                total, same, preferred_element_type=jnp.float32, precision=lax.Precision.HIGHEST
            )
            return total[0:1] * (1.0 / cells)

        shifted = conv - group_mean(conv)
        spread = group_mean(shifted * shifted)
        scaled = shifted * (gain[...] / jnp.sqrt(spread + epsilon)) + shift[...]
        value = scaled / (1.0 + jnp.exp(-scaled))
        for q in range(OF * OH):
            flat[pl.ds(q * OW, OW), :] = value[q * ROW : q * ROW + OW, :]
        out[0] = flat[...].astype(jnp.bfloat16)

    @pl.when(tile >= live)
    def _():
        out[...] = jnp.zeros_like(out)


def decode(panels, idx, count, weight, conv_bias, norm_gain, norm_shift, tiles, slots):
    channels = panels.shape[2]
    whole = lambda t, *_: (0, 0)
    spec = pltpu.PrefetchScalarGridSpec(
        num_scalar_prefetch=2,
        grid=(tiles,),
        in_specs=[
            pl.BlockSpec(memory_space=pl.ANY),
            pl.BlockSpec(weight.shape, lambda t, *_: (0, 0, 0), pipeline_mode=pl.Buffered(1)),
            pl.BlockSpec((1, C_OUT), whole),
            pl.BlockSpec((1, C_OUT), whole),
            pl.BlockSpec((1, C_OUT), whole),
        ],
        out_specs=pl.BlockSpec((1, OCELLS, C_OUT), lambda t, *_: (t, 0, 0)),
        scratch_shapes=[
            pltpu.VMEM((2, slots, PH * PW, channels), jnp.bfloat16),
            pltpu.VMEM((WT, GH * PH * ROW, channels), jnp.bfloat16),
            pltpu.VMEM((MROWS, 9 * channels), jnp.bfloat16),
            pltpu.VMEM((OCELLS, C_OUT), jnp.float32),
            pltpu.SemaphoreType.DMA((2,)),
        ],
    )
    return pl.pallas_call(
        decode_kernel,
        out_shape=jax.ShapeDtypeStruct((tiles, OCELLS, C_OUT), jnp.bfloat16),
        grid_spec=spec,
        compiler_params=pltpu.CompilerParams(vmem_limit_bytes=40 * 2**20),
    )(
        idx,
        count,
        panels,
        weight,
        conv_bias.reshape(1, C_OUT),
        norm_gain.reshape(1, C_OUT),
        norm_shift.reshape(1, C_OUT),
    )


def body(panels, tile_panels, tile_count, conv_weight, conv_bias, norm_gain, norm_shift):
    devices = lax.axis_size("dec")
    tiles, slots = tile_panels.shape
    channels = panels.shape[2]
    weight = conv_weight.transpose(2, 0, 1, 3, 4).reshape(3, 9 * channels, C_OUT)
    if devices <= 16:
        held = lax.all_gather(panels, "dec", axis=0, tiled=True)
        idx = tile_panels.reshape(-1)
    else:
        capacity = max(1, tiles * slots // devices)
        held, idx = fetch_panels(panels, tile_panels, tile_count[0], capacity)
    return decode(
        held, idx, tile_count, weight, conv_bias, norm_gain, norm_shift, tiles, slots
    )


def solution(mesh):
    in_specs = (
        P(("groups", "dec"), None, None),
        P(("groups", "dec"), None),
        P(("groups", "dec")),
        P(),
        P(),
        P(),
        P(),
    )
    out_specs = P(("groups", "dec"), None, None)
    return jax.shard_map(body, mesh=mesh, in_specs=in_specs, out_specs=out_specs, check_vma=False)
```

```python
import jax
import jax.numpy as jnp
from jax import lax
from jax.experimental import pallas as pl
from jax.experimental.pallas import tpu as pltpu
from jax.sharding import PartitionSpec as P

C_OUT = 256
GROUPS = 32
PH = 8
PW = 8
GH = 2
GW = 2
WT = 4
OCELLS = 392
ROW = GW * PW
OH = GH * PH - 2
OW = GW * PW - 2
OF = WT - 2
MROWS = OF * OH * ROW

epsilon = 1e-06


def pick_kernel(rows, panels, out, sem):
    count = out.shape[0]
    for i in range(count):
        pltpu.make_async_copy(panels.at[rows[i]], out.at[i], sem).start()
    pltpu.make_async_copy(out, out, sem).wait()


def pick_rows(panels, rows):
    return pl.pallas_call(
        pick_kernel,
        out_shape=jax.ShapeDtypeStruct((rows.shape[0], *panels.shape[1:]), panels.dtype),
        grid_spec=pltpu.PrefetchScalarGridSpec(
            num_scalar_prefetch=1,
            grid=(1,),
            in_specs=[pl.BlockSpec(memory_space=pl.ANY)],
            out_specs=pl.BlockSpec(memory_space=pl.ANY),
            scratch_shapes=[pltpu.SemaphoreType.DMA],
        ),
    )(rows, panels)


def fetch_panels(panels, work_rows, live_tiles, capacity):
    devices = lax.axis_size("dec")
    per_device = panels.shape[0]
    tile_rows, slot_count = work_rows.shape
    wanted = work_rows.reshape(tile_rows * slot_count)
    ref_live = jnp.arange(tile_rows * slot_count, dtype=jnp.int32) // slot_count < live_tiles
    owner_dev = wanted // per_device
    local_row = wanted % per_device
    order = jnp.arange(tile_rows * slot_count, dtype=jnp.int32)
    earlier = (owner_dev[:, None] == owner_dev[None, :]) & (order[None, :] < order[:, None])
    slot_rank = jnp.sum(earlier.astype(jnp.int32), axis=1)
    where_to = owner_dev * capacity + slot_rank
    places = jnp.arange(devices * capacity, dtype=jnp.int32)
    here = (where_to[None, :] == places[:, None]) & ref_live[None, :]
    request = jnp.sum(jnp.where(here, local_row[None, :], 0), axis=1)
    asked_rows = lax.all_to_all(
        request.reshape(devices, capacity), "dec", split_axis=0, concat_axis=0, tiled=True
    )
    picked = pick_rows(panels, asked_rows.reshape(-1))
    picked = picked.reshape(devices, capacity, *panels.shape[1:])
    returned = lax.all_to_all(picked, "dec", split_axis=0, concat_axis=0, tiled=True)
    landed = returned.reshape(devices * capacity, panels.shape[1], panels.shape[2])
    return landed, jnp.where(ref_live, where_to, 0)


def decode_kernel(idx, count, panels, weight, bias, gain, shift, out, stage, win, cols, flat, sems):
    tile = pl.program_id(0)
    slots = stage.shape[1]
    live = count[0]

    def fetch(which, slot):
        for s in range(slots):
            pltpu.make_async_copy(
                panels.at[idx[which * slots + s]], stage.at[slot, s], sems.at[slot]
            ).start()

    @pl.when(tile == 0)
    def _():
        fetch(0, 0)

    @pl.when(tile + 1 < live)
    def _():
        fetch(tile + 1, (tile + 1) % 2)

    @pl.when(tile < live)
    def _():
        slot = tile % 2
        pltpu.make_async_copy(stage.at[slot], stage.at[slot], sems.at[slot]).wait()
        channels = stage.shape[3]
        for f in range(WT):
            for g in range(GH):
                halves = [
                    stage[slot, (f * GH + g) * GW + h].astype(jnp.float32).reshape(PH, PW, channels)
                    for h in range(GW)
                ]
                rows = jnp.concatenate(halves, axis=1).reshape(PH * ROW, channels)
                win[f, pl.ds(g * PH * ROW, PH * ROW), :] = rows.astype(jnp.bfloat16)
        for a in range(3):
            for b in range(3):
                for f in range(OF):
                    cols[pl.ds(f * OH * ROW, OH * ROW), pl.ds((a * 3 + b) * channels, channels)] = win[
                        f + a, pl.ds(b * ROW, OH * ROW), :
                    ]
        conv = jnp.dot(cols[...], weight[0], preferred_element_type=jnp.float32)
        for c in (1, 2):
            part = jnp.dot(cols[...], weight[c], preferred_element_type=jnp.float32)
            conv = conv + pltpu.roll(part, MROWS - c, 0)
        conv = conv + bias[...]
        column = lax.broadcasted_iota(jnp.int32, (MROWS, C_OUT), 0) % ROW
        valid = column < OW
        lane = lax.broadcasted_iota(jnp.int32, (C_OUT, C_OUT), 0) // (C_OUT // GROUPS)
        other = lax.broadcasted_iota(jnp.int32, (C_OUT, C_OUT), 1) // (C_OUT // GROUPS)
        same = jnp.where(lane == other, 1.0, 0.0).astype(jnp.float32)
        cells = OCELLS * (C_OUT // GROUPS)

        def group_mean(x):
            total = jnp.sum(jnp.where(valid, x, 0.0), axis=0, keepdims=True)
            total = jnp.broadcast_to(total, (8, C_OUT))
            total = jnp.dot(
                total, same, preferred_element_type=jnp.float32, precision=lax.Precision.HIGHEST
            )
            return total[0:1] * (1.0 / cells)

        shifted = conv - group_mean(conv)
        spread = group_mean(shifted * shifted)
        scaled = shifted * (gain[...] / jnp.sqrt(spread + epsilon)) + shift[...]
        value = scaled / (1.0 + jnp.exp(-scaled))
        for q in range(OF * OH):
            flat[pl.ds(q * OW, OW), :] = value[q * ROW : q * ROW + OW, :]
        out[0] = flat[...].astype(jnp.bfloat16)

    @pl.when(tile >= live)
    def _():
        out[...] = jnp.zeros_like(out)


def decode(panels, idx, count, weight, conv_bias, norm_gain, norm_shift, tiles, slots):
    channels = panels.shape[2]
    whole = lambda t, *_: (0, 0)
    spec = pltpu.PrefetchScalarGridSpec(
        num_scalar_prefetch=2,
        grid=(tiles,),
        in_specs=[
            pl.BlockSpec(memory_space=pl.ANY),
            pl.BlockSpec(weight.shape, lambda t, *_: (0, 0, 0), pipeline_mode=pl.Buffered(1)),
            pl.BlockSpec((1, C_OUT), whole),
            pl.BlockSpec((1, C_OUT), whole),
            pl.BlockSpec((1, C_OUT), whole),
        ],
        out_specs=pl.BlockSpec((1, OCELLS, C_OUT), lambda t, *_: (t, 0, 0)),
        scratch_shapes=[
            pltpu.VMEM((2, slots, PH * PW, channels), jnp.bfloat16),
            pltpu.VMEM((WT, GH * PH * ROW, channels), jnp.bfloat16),
            pltpu.VMEM((MROWS, 9 * channels), jnp.bfloat16),
            pltpu.VMEM((OCELLS, C_OUT), jnp.float32),
            pltpu.SemaphoreType.DMA((2,)),
        ],
    )
    return pl.pallas_call(
        decode_kernel,
        out_shape=jax.ShapeDtypeStruct((tiles, OCELLS, C_OUT), jnp.bfloat16),
        grid_spec=spec,
        compiler_params=pltpu.CompilerParams(vmem_limit_bytes=40 * 2**20),
    )(
        idx,
        count,
        panels,
        weight,
        conv_bias.reshape(1, C_OUT),
        norm_gain.reshape(1, C_OUT),
        norm_shift.reshape(1, C_OUT),
    )


def body(panels, tile_panels, tile_count, conv_weight, conv_bias, norm_gain, norm_shift):
    devices = lax.axis_size("dec")
    tiles, slots = tile_panels.shape
    channels = panels.shape[2]
    weight = conv_weight.transpose(2, 0, 1, 3, 4).reshape(3, 9 * channels, C_OUT)
    capacity = max(1, tiles * slots // devices)
    held, idx = fetch_panels(panels, tile_panels, tile_count[0], capacity)
    return decode(
        held, idx, tile_count, weight, conv_bias, norm_gain, norm_shift, tiles, slots
    )


def solution(mesh):
    in_specs = (
        P(("groups", "dec"), None, None),
        P(("groups", "dec"), None),
        P(("groups", "dec")),
        P(),
        P(),
        P(),
        P(),
    )
    out_specs = P(("groups", "dec"), None, None)
    return jax.shard_map(body, mesh=mesh, in_specs=in_specs, out_specs=out_specs, check_vma=False)
```
